32 devices in a mesh: snap: 4 (over x, core), slab: 8 (over z, y).
Axes of the slice: x: 2, y: 2, z: 4, core: 2. Of those that a mesh axis runs over, the one named last changes fastest.
Arguments:
- velocity: bfloat16 [256, 3, 40, 8, 128], P('snap', None, 'slab'), may hold values from -10 to 10
Outputs:
- modes: bfloat16 [768, 8, 5120], P(None, 'slab', 'snap')
- factor: float32 [768, 768], replicated
The draws below stay inside these ranges and needn't reach their ends.
All inputs are finite; a program needn't handle non-finite values.
Results may differ from the reference program's by a relative error of at most 0.0004.
The reference program's roundings to bfloat16 on the way count: a program that leaves them out, or rounds other values in their place, can miss the bound.
Values may be sent and summed in bfloat16 or wider, within the bound.
A program may use at most 64 MiB of HBM per device.

```python
import math
import jax
import jax.numpy as jnp
from jax import lax

SNAPS = 256
CX = 5
Y = 8
Z = 128
NX = 40
POINTS = 40960
N_SLAB = 8


def draw_velocity(key, part):
    groups = SNAPS // 4
    amp_x = 0.5 + jnp.arange(NX, dtype=jnp.float32) / NX
    scale_key = jax.random.fold_in(key, 7)
    amp_s = jnp.exp(jax.random.uniform(scale_key, (SNAPS,), minval=math.log(0.6), maxval=math.log(1.6)))

    def one_group(index):
        group_key = jax.random.fold_in(key, index + 11)
        key_own, key_shared = jax.random.split(group_key)
        own = jnp.clip(jax.random.normal(key_own, (4, 3, NX, Y, Z)), -4.0, 4.0)
        shared = jnp.clip(jax.random.normal(key_shared, (1, 3, NX, Y, Z)), -4.0, 4.0)
        scales = lax.dynamic_slice_in_dim(amp_s, index * 4, 4, 0)
        field = (own + 0.7 * shared) * amp_x[None, None, :, None, None]
        field = field * scales[:, None, None, None, None] * 0.6
        return field.astype(jnp.bfloat16)
    drawn = lax.map(one_group, jnp.arange(groups, dtype=jnp.int32))
    return drawn.reshape(SNAPS, 3, NX, Y, Z)


def setup_inputs(seed: int = 0) -> dict:
    streams_of = jax.random.split(jax.random.key(seed), 2)
    return {
        "velocity": draw_velocity(jax.random.fold_in(streams_of[1], 71), 0),
    }


stencil_weights = (4.0 / 5.0, -1.0 / 5.0, 4.0 / 105.0, -1.0 / 280.0)

def differ(padded, axis, length):
    total = None
    for offset in range(4):
        step = offset + 1
        ahead = lax.slice_in_dim(padded, 4 + step, 4 + step + length, axis=axis)
        behind = lax.slice_in_dim(padded, 4 - step, 4 - step + length, axis=axis)
        term = stencil_weights[offset] * (ahead - behind)
        total = term if total is None else total + term
    return total

def derive(field, axis):
    widths = [(0, 0)] * field.ndim
    widths[axis] = (4, 4)
    return differ(jnp.pad(field, widths), axis, field.shape[axis])

def vorticity_of(snapshot):
    field = snapshot.astype(jnp.float32)
    first, second, third = (field[0], field[1], field[2])
    omega_one = derive(third, 1) - derive(second, 2)
    omega_two = derive(first, 2) - derive(third, 0)
    omega_three = derive(second, 0) - derive(first, 1)
    return jnp.stack([omega_one, omega_two, omega_three], axis=0).astype(jnp.bfloat16)

def reference(velocity):
    vorticity = lax.map(vorticity_of, velocity)
    width = 3 * SNAPS
    planes = vorticity.reshape(width, NX, Y * Z)

    def add_plane(index, total):
        plane = lax.dynamic_slice_in_dim(planes, index, 1, 1)[:, 0, :]
        return total + jnp.dot(plane.astype(jnp.float32), plane.T.astype(jnp.float32), preferred_element_type=jnp.float32)
    gram = lax.fori_loop(0, NX, add_plane, jnp.zeros((width, width), jnp.float32))
    lower = jnp.linalg.cholesky(gram / POINTS)
    factor = lower.T

    def solve_plane(index, result):
        plane = lax.dynamic_slice_in_dim(planes, index, 1, 1)[:, 0, :]
        block = jax.scipy.linalg.solve_triangular(lower, plane.astype(jnp.float32), lower=True)
        return lax.dynamic_update_slice_in_dim(result, block.astype(jnp.bfloat16)[:, None, :], index, 1)
    solved = lax.fori_loop(0, NX, solve_plane, jnp.zeros((width, NX, Y * Z), jnp.bfloat16))
    modes = solved.reshape(width, N_SLAB, CX * Y * Z)
    return (modes, factor)
```

```python
import functools
import jax
import jax.numpy as jnp
from jax import lax
from jax.experimental import pallas as pl
from jax.experimental.pallas import tpu as pltpu
from jax.sharding import PartitionSpec as P

stencil_weights = (4.0 / 5.0, -1.0 / 5.0, 4.0 / 105.0, -1.0 / 280.0)
MESH = pl.DeviceIdType.MESH
HI = lax.Precision.HIGHEST
BLOCK = 128
VMEM_LIMIT = 48 * 1024 * 1024


def with_halo(block, sides, width):
    for axis, dim in sides:
        count = lax.axis_size(axis)
        forward = [(i, i + 1) for i in range(count - 1)]
        backward = [(target, source) for source, target in forward]
        low = lax.ppermute(
            lax.slice_in_dim(block, block.shape[dim] - width, None, axis=dim), axis, forward
        )
        high = lax.ppermute(lax.slice_in_dim(block, 0, width, axis=dim), axis, backward)
        block = jnp.concatenate([low, block, high], axis=dim)
    return block


def differ(padded, axis, length):
    total = None
    for offset in range(4):
        step = offset + 1
        ahead = lax.slice_in_dim(padded, 4 + step, 4 + step + length, axis=axis)
        behind = lax.slice_in_dim(padded, 4 - step, 4 - step + length, axis=axis)
        term = stencil_weights[offset] * (ahead - behind)
        total = term if total is None else total + term
    return total


def derive(field, axis):
    widths = [(0, 0)] * field.ndim
    widths[axis] = (4, 4)
    return differ(jnp.pad(field, widths), axis, field.shape[axis])


def upper_offsets(blocks):
    starts, at = [], 0
    for i in range(blocks):
        starts.append(at)
        at += (blocks - i) * BLOCK
    return starts, at


def halving_steps(snap, slab):
    steps = []
    for axis, count in (("snap", snap), ("slab", slab)):
        bit = 1
        while bit < count:
            steps.append((axis, bit))
            bit *= 2
    return steps


def gram_kernel(steps, m_ref, out_ref, acc_ref, landing, send_sem, recv_sem, gather_send, gather_recv):
    width = m_ref.shape[0]
    blocks = width // BLOCK
    total_rows = acc_ref.shape[0]
    place = {"snap": lax.axis_index("snap"), "slab": lax.axis_index("slab")}

    def partner(axis, bit):
        own = place[axis]
        is_high = lax.rem(own // bit, 2)
        return is_high, {**place, axis: own + bit - 2 * bit * is_high}

    def device(where):
        return (where["snap"], where["slab"])

    barrier = pltpu.get_barrier_semaphore()
    for axis, bit in steps:
        pl.semaphore_signal(barrier, 1, device_id=device(partner(axis, bit)[1]), device_id_type=MESH)

    starts, used = upper_offsets(blocks)
    for i in range(blocks):
        tall = lax.dot_general(
            m_ref[i * BLOCK :, :],
            m_ref[i * BLOCK : (i + 1) * BLOCK, :],
            (((1,), (1,)), ((), ())),
            preferred_element_type=jnp.float32,
        )
        acc_ref[starts[i] : starts[i] + (blocks - i) * BLOCK, :] = tall
    if total_rows > used:
        acc_ref[used:, :] = jnp.zeros((total_rows - used, BLOCK), jnp.float32)
    pl.semaphore_wait(barrier, len(steps))

    start, length, at = 0, total_rows, 0
    history = []
    for index, (axis, bit) in enumerate(steps):
        half = length // 2
        is_high, other = partner(axis, bit)
        keep = pl.multiple_of(start + is_high * half, 8)
        give = pl.multiple_of(start + (1 - is_high) * half, 8)
        copy = pltpu.make_async_remote_copy(
            src_ref=acc_ref.at[pl.ds(give, half)],
            dst_ref=landing.at[pl.ds(at, half)],
            send_sem=send_sem.at[index],
            recv_sem=recv_sem.at[index],
            device_id=device(other),
            device_id_type=MESH,
        )
        copy.start()
        copy.wait()
        acc_ref[pl.ds(keep, half), :] = acc_ref[pl.ds(keep, half), :] + landing[at : at + half, :]
        history.append((index, axis, bit, keep, half))
        start, length, at = keep, half, at + half
    out_ref[pl.ds(start, length), :] = acc_ref[pl.ds(start, length), :]
    for index, axis, bit, keep, half in reversed(history):
        other = partner(axis, bit)[1]
        copy = pltpu.make_async_remote_copy(
            src_ref=out_ref.at[pl.ds(keep, half)],
            dst_ref=out_ref.at[pl.ds(keep, half)],
            send_sem=gather_send.at[index],
            recv_sem=gather_recv.at[index],
            device_id=device(other),
            device_id_type=MESH,
        )
        copy.start()
        copy.wait()


def summed_gram(matrix, snap, slab):
    width, points = matrix.shape
    used = upper_offsets(width // BLOCK)[1]
    devices = snap * slab
    share = -(-used // (devices * 8)) * 8
    rows = share * devices
    steps = halving_steps(snap, slab)
    count = max(len(steps), 1)
    return pl.pallas_call(
        functools.partial(gram_kernel, steps),
        out_shape=jax.ShapeDtypeStruct((rows, BLOCK), jnp.float32),
        in_specs=[pl.BlockSpec(memory_space=pltpu.VMEM)],
        out_specs=pl.BlockSpec(memory_space=pltpu.VMEM),
        scratch_shapes=[
            pltpu.VMEM((rows, BLOCK), jnp.float32),
            pltpu.VMEM((rows, BLOCK), jnp.float32),
            pltpu.SemaphoreType.DMA((count,)),
            pltpu.SemaphoreType.DMA((count,)),
            pltpu.SemaphoreType.DMA((count,)),
            pltpu.SemaphoreType.DMA((count,)),
        ],
        compiler_params=pltpu.CompilerParams(
            collective_id=1, has_side_effects=True, vmem_limit_bytes=VMEM_LIMIT
        ),
        name="gram_sum",
    )(matrix)


def factor_diagonal(d_ref, w_ref, out_ref, spread):
    group = 8
    count = BLOCK // group
    for g in range(count):
        lo = g * group
        tile = d_ref[lo : lo + group, :]
        for k in range(group):
            spread[g % 2, k] = jnp.broadcast_to(tile[:, lo + k : lo + k + 1], (group, BLOCK))
        a = [[spread[g % 2, k, i : i + 1, :] for k in range(i + 1)] for i in range(group)]
        mult = [[None] * group for _ in range(group)]
        inv = [None] * group
        root = [None] * group
        for k in range(group):
            inv[k] = 1.0 / a[k][k]
            root[k] = lax.rsqrt(a[k][k])
            for i in range(k + 1, group):
                mult[i][k] = a[i][k] * inv[k]
            for i in range(k + 1, group):
                for j in range(k + 1, i + 1):
                    a[i][j] = a[i][j] - mult[i][k] * a[j][k]
        rows = [d_ref[lo + i : lo + i + 1, :] for i in range(group)]
        sides = [w_ref[lo + i : lo + i + 1, :] for i in range(group)]
        for k in range(group):
            for i in range(k + 1, group):
                rows[i] = rows[i] - mult[i][k] * rows[k]
                sides[i] = sides[i] - mult[i][k] * sides[k]
        for i in range(group):
            out_ref[lo + i : lo + i + 1, :] = sides[i] * root[i]
        for t in range(g + 1, count):
            below = d_ref[t * group : (t + 1) * group, :]
            aside = w_ref[t * group : (t + 1) * group, :]
            columns = [
                jnp.broadcast_to(below[:, lo + k : lo + k + 1], (group, BLOCK)) for k in range(group)
            ]
            for k in range(group):
                for i in range(k + 1, group):
                    columns[i] = columns[i] - mult[i][k] * columns[k]
            for k in range(group):
                scaled = columns[k] * inv[k]
                below = below - scaled * rows[k]
                aside = aside - scaled * sides[k]
            d_ref[t * group : (t + 1) * group, :] = below
            w_ref[t * group : (t + 1) * group, :] = aside


def solve_kernel(points, g_ref, m_ref, modes_ref, factor_ref, work, inverse, diag, side, dinv, spread):
    width = m_ref.shape[0]
    blocks = width // BLOCK
    starts, _ = upper_offsets(blocks)
    rank = lax.broadcasted_iota(jnp.int32, (BLOCK, BLOCK), 0)
    lane = lax.broadcasted_iota(jnp.int32, (BLOCK, BLOCK), 1)
    eye = jnp.where(rank == lane, 1.0, 0.0).astype(jnp.float32)
    zero = jnp.zeros((BLOCK, BLOCK), jnp.float32)
    for i in range(blocks):
        for j in range(blocks):
            here = (slice(i * BLOCK, (i + 1) * BLOCK), slice(j * BLOCK, (j + 1) * BLOCK))
            there = (here[0], slice(width + j * BLOCK, width + (j + 1) * BLOCK))
            if j >= i:
                row = starts[i] + (j - i) * BLOCK
                block = g_ref[row : row + BLOCK, :] / points
                work[here] = block if i == j else block.T
            else:
                work[here] = zero
            work[there] = eye if i == j else zero

    def step(k, carry):
        base = pl.multiple_of(k * BLOCK, BLOCK)
        diag[...] = work[pl.ds(base, BLOCK), pl.ds(base, BLOCK)]
        side[...] = eye
        factor_diagonal(diag, side, dinv, spread)
        panel = jnp.dot(
            dinv[...], work[pl.ds(base, BLOCK), :], precision=HI, preferred_element_type=jnp.float32
        )
        work[pl.ds(base, BLOCK), :] = panel

        def update(i, inner):
            low = pl.multiple_of(i * BLOCK, BLOCK)
            left = work[pl.ds(base, BLOCK), pl.ds(low, BLOCK)].T
            work[pl.ds(low, BLOCK), :] -= jnp.dot(
                left, work[pl.ds(base, BLOCK), :], precision=HI, preferred_element_type=jnp.float32
            )
            return inner

        lax.fori_loop(k + 1, blocks, update, 0)
        return carry

    lax.fori_loop(0, blocks, step, 0)
    for i in range(blocks):
        rows = slice(i * BLOCK, (i + 1) * BLOCK)
        for j in range(blocks):
            cols = slice(j * BLOCK, (j + 1) * BLOCK)
            if j < i:
                factor_ref[rows, cols] = zero
            elif j == i:
                factor_ref[rows, cols] = jnp.where(lane >= rank, work[rows, cols], 0.0)
            else:
                factor_ref[rows, cols] = work[rows, cols]
        depth = (i + 1) * BLOCK
        part = work[rows, width : width + depth]
        top = part.astype(jnp.bfloat16)
        rest = (part - top.astype(jnp.float32)).astype(jnp.bfloat16)
        solved = jnp.dot(top, m_ref[:depth, :], preferred_element_type=jnp.float32)
        solved = solved + jnp.dot(rest, m_ref[:depth, :], preferred_element_type=jnp.float32)
        modes_ref[rows, :] = solved.astype(jnp.bfloat16)


def factor_and_solve(gram, matrix, points):
    width, count = matrix.shape
    vmem = pl.BlockSpec(memory_space=pltpu.VMEM)
    return pl.pallas_call(
        functools.partial(solve_kernel, float(points)),
        out_shape=(
            jax.ShapeDtypeStruct((width, count), jnp.bfloat16),
            jax.ShapeDtypeStruct((width, width), jnp.float32),
        ),
        in_specs=[vmem, vmem],
        out_specs=(vmem, vmem),
        scratch_shapes=[
            pltpu.VMEM((width, 2 * width), jnp.float32),
            pltpu.VMEM((8, BLOCK), jnp.float32),
            pltpu.VMEM((BLOCK, BLOCK), jnp.float32),
            pltpu.VMEM((BLOCK, BLOCK), jnp.float32),
            pltpu.VMEM((BLOCK, BLOCK), jnp.float32),
            pltpu.VMEM((2, 8, 8, BLOCK), jnp.float32),
        ],
        compiler_params=pltpu.CompilerParams(vmem_limit_bytes=VMEM_LIMIT),
        name="factor_solve",
    )(gram, matrix)


def body(velocity):
    planes = velocity.shape[2]
    extended = with_halo(velocity[:, 1:3], (("slab", 2),), 4)
    second_rim = extended[:, 0].astype(jnp.float32)
    third_rim = extended[:, 1].astype(jnp.float32)
    first = velocity[:, 0].astype(jnp.float32)
    second = velocity[:, 1].astype(jnp.float32)
    third = velocity[:, 2].astype(jnp.float32)
    omega_one = derive(third, 2) - derive(second, 3)
    omega_two = derive(first, 3) - differ(third_rim, 1, planes)
    omega_three = differ(second_rim, 1, planes) - derive(first, 2)
    vorticity = jnp.stack([omega_one, omega_two, omega_three], axis=1).astype(jnp.bfloat16)
    local_snaps = vorticity.shape[0]
    flat = vorticity.reshape(local_snaps, 3, -1)
    regrouped = lax.all_to_all(flat, "snap", split_axis=2, concat_axis=0, tiled=True)
    width = regrouped.shape[0] * 3
    matrix = regrouped.reshape(width, -1)
    rows = matrix.shape[1]
    snap, slab = lax.axis_size("snap"), lax.axis_size("slab")
    total = summed_gram(matrix, snap, slab)
    modes, factor = factor_and_solve(total, matrix, rows * snap * slab)
    return (modes.reshape(width, 1, rows), factor)


def solution(mesh):
    in_specs = (P("snap", None, "slab", None, None),)
    out_specs = (P(None, "slab", "snap"), P())
    return jax.shard_map(body, mesh=mesh, in_specs=in_specs, out_specs=out_specs, check_vma=False)
```

```python
import functools
import jax
import jax.numpy as jnp
from jax import lax
from jax.experimental import pallas as pl
from jax.experimental.pallas import tpu as pltpu
from jax.sharding import PartitionSpec as P

stencil_weights = (4.0 / 5.0, -1.0 / 5.0, 4.0 / 105.0, -1.0 / 280.0)
MESH = pl.DeviceIdType.MESH
HI = lax.Precision.HIGHEST
BLOCK = 128
VMEM_LIMIT = 48 * 1024 * 1024


def with_halo(block, sides, width):
    for axis, dim in sides:
        count = lax.axis_size(axis)
        forward = [(i, i + 1) for i in range(count - 1)]
        backward = [(target, source) for source, target in forward]
        low = lax.ppermute(
            lax.slice_in_dim(block, block.shape[dim] - width, None, axis=dim), axis, forward
        )
        high = lax.ppermute(lax.slice_in_dim(block, 0, width, axis=dim), axis, backward)
        block = jnp.concatenate([low, block, high], axis=dim)
    return block


def differ(padded, axis, length):
    total = None
    for offset in range(4):
        step = offset + 1
        ahead = lax.slice_in_dim(padded, 4 + step, 4 + step + length, axis=axis)
        behind = lax.slice_in_dim(padded, 4 - step, 4 - step + length, axis=axis)
        term = stencil_weights[offset] * (ahead - behind)
        total = term if total is None else total + term
    return total


def derive(field, axis):
    widths = [(0, 0)] * field.ndim
    widths[axis] = (4, 4)
    return differ(jnp.pad(field, widths), axis, field.shape[axis])


def upper_offsets(blocks):
    starts, at = [], 0
    for i in range(blocks):
        starts.append(at)
        at += (blocks - i) * BLOCK
    return starts, at


def halving_steps(snap, slab):
    steps = []
    for axis, count in (("snap", snap), ("slab", slab)):
        bit = 1
        while bit < count:
            steps.append((axis, bit))
            bit *= 2
    return steps


def gram_kernel(
    sizes, streams, f_ref, m_ref, out_ref, acc_ref, landing,
    send_sem, recv_sem, gather_send, gather_recv, move_send, move_recv, own_sem,
):
    width, columns = m_ref.shape
    blocks = width // BLOCK
    height = f_ref.shape[0]
    total_rows = acc_ref.shape[0]
    place = {"snap": lax.axis_index("snap"), "slab": lax.axis_index("slab")}

    def partner(axis, bit):
        own = place[axis]
        is_high = lax.rem(own // bit, 2)
        return is_high, {**place, axis: own + bit - 2 * bit * is_high}

    def device(where):
        return (where["snap"], where["slab"])

    others = [
        {**place, "snap": lax.rem(place["snap"] + d, sizes["snap"])} for d in range(1, sizes["snap"])
    ]
    greeted = others + [partner(axis, bit)[1] for axis, bit in streams[0] if axis == "slab"]
    barrier = pltpu.get_barrier_semaphore()
    for where in greeted:
        pl.semaphore_signal(barrier, 1, device_id=device(where), device_id_type=MESH)
    pl.semaphore_wait(barrier, len(greeted))

    own_rows = pl.ds(pl.multiple_of(place["snap"] * height, 16), height)
    moves = []
    for d, where in enumerate(others):
        strip = pl.ds(pl.multiple_of(where["snap"] * columns, BLOCK), columns)
        move = pltpu.make_async_remote_copy(
            src_ref=f_ref.at[:, strip],
            dst_ref=m_ref.at[own_rows, :],
            send_sem=move_send.at[d],
            recv_sem=move_recv.at[d],
            device_id=device(where),
            device_id_type=MESH,
        )
        move.start()
        moves.append(move)
    own_strip = pl.ds(pl.multiple_of(place["snap"] * columns, BLOCK), columns)
    stay = pltpu.make_async_copy(f_ref.at[:, own_strip], m_ref.at[own_rows, :], own_sem)
    stay.start()
    stay.wait()
    for move in moves:
        move.wait()

    starts, used = upper_offsets(blocks)
    for i in range(blocks):
        tall = lax.dot_general(
            m_ref[i * BLOCK :, :],
            m_ref[i * BLOCK : (i + 1) * BLOCK, :],
            (((1,), (1,)), ((), ())),
            preferred_element_type=jnp.float32,
        )
        acc_ref[starts[i] : starts[i] + (blocks - i) * BLOCK, :] = tall
    if total_rows > used:
        acc_ref[used:, :] = jnp.zeros((total_rows - used, BLOCK), jnp.float32)

    lane_rows = total_rows // len(streams)
    state = [(t * lane_rows, lane_rows, t * lane_rows) for t in range(len(streams))]
    history = []
    for index in range(len(streams[0])):
        flying = []
        for t, steps in enumerate(streams):
            axis, bit = steps[index]
            start, length, at = state[t]
            half = length // 2
            is_high, other = partner(axis, bit)
            keep = pl.multiple_of(start + is_high * half, 8)
            give = pl.multiple_of(start + (1 - is_high) * half, 8)
            copy = pltpu.make_async_remote_copy(
                src_ref=acc_ref.at[pl.ds(give, half)],
                dst_ref=landing.at[pl.ds(at, half)],
                send_sem=send_sem.at[t, index],
                recv_sem=recv_sem.at[t, index],
                device_id=device(other),
                device_id_type=MESH,
            )
            copy.start()
            flying.append((copy, keep, half, at))
            state[t] = (keep, half, at + half)
        for copy, keep, half, at in flying:
            copy.wait()
            acc_ref[pl.ds(keep, half), :] = acc_ref[pl.ds(keep, half), :] + landing[at : at + half, :]
        history.append([(keep, half) for _, keep, half, _ in flying])
    for start, length, _ in state:
        out_ref[pl.ds(start, length), :] = acc_ref[pl.ds(start, length), :]
    for index in reversed(range(len(streams[0]))):
        flying = []
        for t, steps in enumerate(streams):
            axis, bit = steps[index]
            keep, half = history[index][t]
            copy = pltpu.make_async_remote_copy(
                src_ref=out_ref.at[pl.ds(keep, half)],
                dst_ref=out_ref.at[pl.ds(keep, half)],
                send_sem=gather_send.at[t, index],
                recv_sem=gather_recv.at[t, index],
                device_id=device(partner(axis, bit)[1]),
                device_id_type=MESH,
            )
            copy.start()
            flying.append(copy)
        for copy in flying:
            copy.wait()


def summed_gram(flat, snap, slab):
    height, points = flat.shape
    width, columns = height * snap, points // snap
    used = upper_offsets(width // BLOCK)[1]
    devices = snap * slab
    steps = halving_steps(snap, slab)
    lead, rest = steps[:1], steps[1:]
    shifts = (0, len(halving_steps(snap, 1)) - 1, len(halving_steps(snap, 1)))
    streams = [lead + rest[shift:] + rest[:shift] for shift in shifts]
    share = -(-used // (len(streams) * devices * 8)) * 8
    rows = share * devices * len(streams)
    vmem = pl.BlockSpec(memory_space=pltpu.VMEM)
    stages = pltpu.SemaphoreType.DMA((len(streams), len(steps)))
    moves = pltpu.SemaphoreType.DMA((snap,))
    return pl.pallas_call(
        functools.partial(gram_kernel, {"snap": snap, "slab": slab}, streams),
        out_shape=(
            jax.ShapeDtypeStruct((width, columns), flat.dtype),
            jax.ShapeDtypeStruct((rows, BLOCK), jnp.float32),
        ),
        in_specs=[vmem],
        out_specs=(vmem, vmem),
        scratch_shapes=[
            pltpu.VMEM((rows, BLOCK), jnp.float32),
            pltpu.VMEM((rows, BLOCK), jnp.float32),
            stages, stages, stages, stages,
            moves, moves,
            pltpu.SemaphoreType.DMA,
        ],
        compiler_params=pltpu.CompilerParams(
            collective_id=1, has_side_effects=True, vmem_limit_bytes=VMEM_LIMIT
        ),
        name="gram_sum",
    )(flat)


def factor_diagonal(d_ref, w_ref, out_ref, spread):
    group = 8
    count = BLOCK // group
    for g in range(count):
        lo = g * group
        tile = d_ref[lo : lo + group, :]
        for k in range(group):
            spread[g % 2, k] = jnp.broadcast_to(tile[:, lo + k : lo + k + 1], (group, BLOCK))
        a = [[spread[g % 2, k, i : i + 1, :] for k in range(i + 1)] for i in range(group)]
        mult = [[None] * group for _ in range(group)]
        inv = [None] * group
        root = [None] * group
        for k in range(group):
            inv[k] = 1.0 / a[k][k]
            root[k] = lax.rsqrt(a[k][k])
            for i in range(k + 1, group):
                mult[i][k] = a[i][k] * inv[k]
            for i in range(k + 1, group):
                for j in range(k + 1, i + 1):
                    a[i][j] = a[i][j] - mult[i][k] * a[j][k]
        rows = [d_ref[lo + i : lo + i + 1, :] for i in range(group)]
        sides = [w_ref[lo + i : lo + i + 1, :] for i in range(group)]
        for k in range(group):
            for i in range(k + 1, group):
                rows[i] = rows[i] - mult[i][k] * rows[k]
                sides[i] = sides[i] - mult[i][k] * sides[k]
        for i in range(group):
            out_ref[lo + i : lo + i + 1, :] = sides[i] * root[i]
        for t in range(g + 1, count):
            below = d_ref[t * group : (t + 1) * group, :]
            aside = w_ref[t * group : (t + 1) * group, :]
            columns = [
                jnp.broadcast_to(below[:, lo + k : lo + k + 1], (group, BLOCK)) for k in range(group)
            ]
            for k in range(group):
                for i in range(k + 1, group):
                    columns[i] = columns[i] - mult[i][k] * columns[k]
            for k in range(group):
                scaled = columns[k] * inv[k]
                below = below - scaled * rows[k]
                aside = aside - scaled * sides[k]
            d_ref[t * group : (t + 1) * group, :] = below
            w_ref[t * group : (t + 1) * group, :] = aside


def solve_kernel(points, g_ref, m_ref, modes_ref, factor_ref, work, inverse, diag, side, dinv, spread):
    width = m_ref.shape[0]
    blocks = width // BLOCK
    starts, _ = upper_offsets(blocks)
    rank = lax.broadcasted_iota(jnp.int32, (BLOCK, BLOCK), 0)
    lane = lax.broadcasted_iota(jnp.int32, (BLOCK, BLOCK), 1)
    eye = jnp.where(rank == lane, 1.0, 0.0).astype(jnp.float32)
    zero = jnp.zeros((BLOCK, BLOCK), jnp.float32)
    for i in range(blocks):
        for j in range(blocks):
            here = (slice(i * BLOCK, (i + 1) * BLOCK), slice(j * BLOCK, (j + 1) * BLOCK))
            there = (here[0], slice(width + j * BLOCK, width + (j + 1) * BLOCK))
            if j >= i:
                row = starts[i] + (j - i) * BLOCK
                block = g_ref[row : row + BLOCK, :] / points
                work[here] = block if i == j else block.T
            else:
                work[here] = zero
            work[there] = eye if i == j else zero

    def step(k, carry):
        base = pl.multiple_of(k * BLOCK, BLOCK)
        diag[...] = work[pl.ds(base, BLOCK), pl.ds(base, BLOCK)]
        side[...] = eye
        factor_diagonal(diag, side, dinv, spread)
        panel = jnp.dot(
            dinv[...], work[pl.ds(base, BLOCK), :], precision=HI, preferred_element_type=jnp.float32
        )
        work[pl.ds(base, BLOCK), :] = panel

        def update(i, inner):
            low = pl.multiple_of(i * BLOCK, BLOCK)
            left = work[pl.ds(base, BLOCK), pl.ds(low, BLOCK)].T
            work[pl.ds(low, BLOCK), :] -= jnp.dot(
                left, work[pl.ds(base, BLOCK), :], precision=HI, preferred_element_type=jnp.float32
            )
            return inner

        lax.fori_loop(k + 1, blocks, update, 0)
        return carry

    lax.fori_loop(0, blocks, step, 0)
    for i in range(blocks):
        rows = slice(i * BLOCK, (i + 1) * BLOCK)
        for j in range(blocks):
            cols = slice(j * BLOCK, (j + 1) * BLOCK)
            if j < i:
                factor_ref[rows, cols] = zero
            elif j == i:
                factor_ref[rows, cols] = jnp.where(lane >= rank, work[rows, cols], 0.0)
            else:
                factor_ref[rows, cols] = work[rows, cols]
        depth = (i + 1) * BLOCK
        part = work[rows, width : width + depth]
        top = part.astype(jnp.bfloat16)
        rest = (part - top.astype(jnp.float32)).astype(jnp.bfloat16)
        solved = jnp.dot(top, m_ref[:depth, :], preferred_element_type=jnp.float32)
        solved = solved + jnp.dot(rest, m_ref[:depth, :], preferred_element_type=jnp.float32)
        modes_ref[rows, :] = solved.astype(jnp.bfloat16)


def factor_and_solve(gram, matrix, points):
    width, count = matrix.shape
    vmem = pl.BlockSpec(memory_space=pltpu.VMEM)
    return pl.pallas_call(
        functools.partial(solve_kernel, float(points)),
        out_shape=(
            jax.ShapeDtypeStruct((width, count), jnp.bfloat16),
            jax.ShapeDtypeStruct((width, width), jnp.float32),
        ),
        in_specs=[vmem, vmem],
        out_specs=(vmem, vmem),
        scratch_shapes=[
            pltpu.VMEM((width, 2 * width), jnp.float32),
            pltpu.VMEM((8, BLOCK), jnp.float32),
            pltpu.VMEM((BLOCK, BLOCK), jnp.float32),
            pltpu.VMEM((BLOCK, BLOCK), jnp.float32),
            pltpu.VMEM((BLOCK, BLOCK), jnp.float32),
            pltpu.VMEM((2, 8, 8, BLOCK), jnp.float32),
        ],
        compiler_params=pltpu.CompilerParams(vmem_limit_bytes=VMEM_LIMIT),
        name="factor_solve",
    )(gram, matrix)


def body(velocity):
    planes = velocity.shape[2]
    extended = with_halo(velocity[:, 1:3], (("slab", 2),), 4)
    second_rim = extended[:, 0].astype(jnp.float32)
    third_rim = extended[:, 1].astype(jnp.float32)
    first = velocity[:, 0].astype(jnp.float32)
    second = velocity[:, 1].astype(jnp.float32)
    third = velocity[:, 2].astype(jnp.float32)
    omega_one = derive(third, 2) - derive(second, 3)
    omega_two = derive(first, 3) - differ(third_rim, 1, planes)
    omega_three = differ(second_rim, 1, planes) - derive(first, 2)
    vorticity = jnp.stack([omega_one, omega_two, omega_three], axis=1).astype(jnp.bfloat16)
    flat = vorticity.reshape(vorticity.shape[0] * 3, -1)
    snap, slab = lax.axis_size("snap"), lax.axis_size("slab")
    matrix, total = summed_gram(flat, snap, slab)
    width, rows = matrix.shape
    modes, factor = factor_and_solve(total, matrix, rows * snap * slab)
    return (modes.reshape(width, 1, rows), factor)


def solution(mesh):
    in_specs = (P("snap", None, "slab", None, None),)
    out_specs = (P(None, "slab", "snap"), P())
    return jax.shard_map(body, mesh=mesh, in_specs=in_specs, out_specs=out_specs, check_vma=False)
```

```python
import functools
import jax
import jax.numpy as jnp
from jax import lax
from jax.experimental import pallas as pl
from jax.experimental.pallas import tpu as pltpu
from jax.sharding import PartitionSpec as P

stencil_weights = (4.0 / 5.0, -1.0 / 5.0, 4.0 / 105.0, -1.0 / 280.0)
MESH = pl.DeviceIdType.MESH
HI = lax.Precision.HIGHEST
BLOCK = 128
VMEM_LIMIT = 48 * 1024 * 1024


def with_halo(block, sides, width):
    for axis, dim in sides:
        count = lax.axis_size(axis)
        forward = [(i, i + 1) for i in range(count - 1)]
        backward = [(target, source) for source, target in forward]
        low = lax.ppermute(
            lax.slice_in_dim(block, block.shape[dim] - width, None, axis=dim), axis, forward
        )
        high = lax.ppermute(lax.slice_in_dim(block, 0, width, axis=dim), axis, backward)
        block = jnp.concatenate([low, block, high], axis=dim)
    return block


def differ(padded, axis, length):
    total = None
    for offset in range(4):
        step = offset + 1
        ahead = lax.slice_in_dim(padded, 4 + step, 4 + step + length, axis=axis)
        behind = lax.slice_in_dim(padded, 4 - step, 4 - step + length, axis=axis)
        term = stencil_weights[offset] * (ahead - behind)
        total = term if total is None else total + term
    return total


def derive(field, axis):
    widths = [(0, 0)] * field.ndim
    widths[axis] = (4, 4)
    return differ(jnp.pad(field, widths), axis, field.shape[axis])


def upper_offsets(blocks):
    starts, at = [], 0
    for i in range(blocks):
        starts.append(at)
        at += (blocks - i) * BLOCK
    return starts, at


def halving_steps(snap, slab):
    steps = []
    for axis, count in (("snap", snap), ("slab", slab)):
        bit = 1
        while bit < count:
            steps.append((axis, bit))
            bit *= 2
    return steps


def gram_kernel(
    sizes, streams, f_ref, m_ref, out_ref, acc_ref, landing,
    send_sem, recv_sem, gather_send, gather_recv, move_send, move_recv, own_sem,
):
    width, columns = m_ref.shape
    blocks = width // BLOCK
    height = f_ref.shape[0]
    total_rows = acc_ref.shape[0]
    place = {"snap": lax.axis_index("snap"), "slab": lax.axis_index("slab")}

    def partner(axis, bit):
        own = place[axis]
        is_high = lax.rem(own // bit, 2)
        return is_high, {**place, axis: own + bit - 2 * bit * is_high}

    def device(where):
        return (where["snap"], where["slab"])

    others = [
        {**place, "snap": lax.rem(place["snap"] + d, sizes["snap"])} for d in range(1, sizes["snap"])
    ]
    greeted = others + [partner(axis, bit)[1] for axis, bit in streams[0] if axis == "slab"]
    barrier = pltpu.get_barrier_semaphore()
    for where in greeted:
        pl.semaphore_signal(barrier, 1, device_id=device(where), device_id_type=MESH)
    pl.semaphore_wait(barrier, len(greeted))

    own_rows = pl.ds(pl.multiple_of(place["snap"] * height, 16), height)
    moves = []
    for d, where in enumerate(others):
        strip = pl.ds(pl.multiple_of(where["snap"] * columns, BLOCK), columns)
        move = pltpu.make_async_remote_copy(
            src_ref=f_ref.at[:, strip],
            dst_ref=m_ref.at[own_rows, :],
            send_sem=move_send.at[d],
            recv_sem=move_recv.at[d],
            device_id=device(where),
            device_id_type=MESH,
        )
        move.start()
        moves.append(move)
    own_strip = pl.ds(pl.multiple_of(place["snap"] * columns, BLOCK), columns)
    stay = pltpu.make_async_copy(f_ref.at[:, own_strip], m_ref.at[own_rows, :], own_sem)
    stay.start()
    stay.wait()
    for move in moves:
        move.wait()

    starts, used = upper_offsets(blocks)
    for i in range(blocks):
        tall = lax.dot_general(
            m_ref[i * BLOCK :, :],
            m_ref[i * BLOCK : (i + 1) * BLOCK, :],
            (((1,), (1,)), ((), ())),
            preferred_element_type=jnp.float32,
        )
        acc_ref[starts[i] : starts[i] + (blocks - i) * BLOCK, :] = tall
    if total_rows > used:
        acc_ref[used:, :] = jnp.zeros((total_rows - used, BLOCK), jnp.float32)

    lane_rows = total_rows // len(streams)
    state = [(t * lane_rows, lane_rows, t * lane_rows) for t in range(len(streams))]
    history = []
    for index in range(len(streams[0])):
        flying = []
        for t, steps in enumerate(streams):
            axis, bit = steps[index]
            start, length, at = state[t]
            half = length // 2
            is_high, other = partner(axis, bit)
            keep = pl.multiple_of(start + is_high * half, 8)
            give = pl.multiple_of(start + (1 - is_high) * half, 8)
            copy = pltpu.make_async_remote_copy(
                src_ref=acc_ref.at[pl.ds(give, half)],
                dst_ref=landing.at[pl.ds(at, half)],
                send_sem=send_sem.at[t, index],
                recv_sem=recv_sem.at[t, index],
                device_id=device(other),
                device_id_type=MESH,
            )
            copy.start()
            flying.append((copy, keep, half, at))
            state[t] = (keep, half, at + half)
        for copy, keep, half, at in flying:
            copy.wait()
            acc_ref[pl.ds(keep, half), :] = acc_ref[pl.ds(keep, half), :] + landing[at : at + half, :]
        history.append([(keep, half) for _, keep, half, _ in flying])
    for start, length, _ in state:
        out_ref[pl.ds(start, length), :] = acc_ref[pl.ds(start, length), :]
    for index in reversed(range(len(streams[0]))):
        flying = []
        for t, steps in enumerate(streams):
            axis, bit = steps[index]
            keep, half = history[index][t]
            copy = pltpu.make_async_remote_copy(
                src_ref=out_ref.at[pl.ds(keep, half)],
                dst_ref=out_ref.at[pl.ds(keep, half)],
                send_sem=gather_send.at[t, index],
                recv_sem=gather_recv.at[t, index],
                device_id=device(partner(axis, bit)[1]),
                device_id_type=MESH,
            )
            copy.start()
            flying.append(copy)
        for copy in flying:
            copy.wait()


def summed_gram(flat, snap, slab):
    height, points = flat.shape
    width, columns = height * snap, points // snap
    used = upper_offsets(width // BLOCK)[1]
    devices = snap * slab
    steps = halving_steps(snap, slab)
    lead, rest = steps[:1], steps[1:]
    shifts = (0, len(halving_steps(snap, 1)) - 1, len(halving_steps(snap, 1)))
    streams = [lead + rest[shift:] + rest[:shift] for shift in shifts]
    share = -(-used // (len(streams) * devices * 8)) * 8
    rows = share * devices * len(streams)
    vmem = pl.BlockSpec(memory_space=pltpu.VMEM)
    stages = pltpu.SemaphoreType.DMA((len(streams), len(steps)))
    moves = pltpu.SemaphoreType.DMA((snap,))
    return pl.pallas_call(
        functools.partial(gram_kernel, {"snap": snap, "slab": slab}, streams),
        out_shape=(
            jax.ShapeDtypeStruct((width, columns), flat.dtype),
            jax.ShapeDtypeStruct((rows, BLOCK), jnp.float32),
        ),
        in_specs=[vmem],
        out_specs=(vmem, vmem),
        scratch_shapes=[
            pltpu.VMEM((rows, BLOCK), jnp.float32),
            pltpu.VMEM((rows, BLOCK), jnp.float32),
            stages, stages, stages, stages,
            moves, moves,
            pltpu.SemaphoreType.DMA,
        ],
        compiler_params=pltpu.CompilerParams(
            collective_id=1, has_side_effects=True, vmem_limit_bytes=VMEM_LIMIT
        ),
        name="gram_sum",
    )(flat)


def factor_diagonal(d_ref, w_ref, out_ref, spread):
    group = 8
    count = BLOCK // group
    for g in range(count):
        lo = g * group
        tile = d_ref[lo : lo + group, :]
        for k in range(group):
            spread[g % 2, k] = jnp.broadcast_to(tile[:, lo + k : lo + k + 1], (group, BLOCK))
        a = [[spread[g % 2, k, i : i + 1, :] for k in range(i + 1)] for i in range(group)]
        mult = [[None] * group for _ in range(group)]
        inv = [None] * group
        root = [None] * group
        for k in range(group):
            inv[k] = 1.0 / a[k][k]
            root[k] = lax.rsqrt(a[k][k])
            for i in range(k + 1, group):
                mult[i][k] = a[i][k] * inv[k]
            for i in range(k + 1, group):
                for j in range(k + 1, i + 1):
                    a[i][j] = a[i][j] - mult[i][k] * a[j][k]
        rows = [d_ref[lo + i : lo + i + 1, :] for i in range(group)]
        sides = [w_ref[lo + i : lo + i + 1, :] for i in range(group)]
        for k in range(group):
            for i in range(k + 1, group):
                rows[i] = rows[i] - mult[i][k] * rows[k]
                sides[i] = sides[i] - mult[i][k] * sides[k]
        for i in range(group):
            out_ref[lo + i : lo + i + 1, :] = sides[i] * root[i]
        for t in range(g + 1, count):
            below = d_ref[t * group : (t + 1) * group, :]
            aside = w_ref[t * group : (t + 1) * group, :]
            columns = [
                jnp.broadcast_to(below[:, lo + k : lo + k + 1], (group, BLOCK)) for k in range(group)
            ]
            for k in range(group):
                for i in range(k + 1, group):
                    columns[i] = columns[i] - mult[i][k] * columns[k]
            for k in range(group):
                scaled = columns[k] * inv[k]
                below = below - scaled * rows[k]
                aside = aside - scaled * sides[k]
            d_ref[t * group : (t + 1) * group, :] = below
            w_ref[t * group : (t + 1) * group, :] = aside


def solve_kernel(points, g_ref, m_ref, modes_ref, factor_ref, work, diag, side, dinv, spread):
    width = m_ref.shape[0]
    blocks = width // BLOCK
    starts, _ = upper_offsets(blocks)
    rank = lax.broadcasted_iota(jnp.int32, (BLOCK, BLOCK), 0)
    lane = lax.broadcasted_iota(jnp.int32, (BLOCK, BLOCK), 1)
    eye = jnp.where(rank == lane, 1.0, 0.0).astype(jnp.float32)
    zero = jnp.zeros((BLOCK, BLOCK), jnp.float32)
    for i in range(blocks):
        for j in range(blocks):
            here = (slice(i * BLOCK, (i + 1) * BLOCK), slice(j * BLOCK, (j + 1) * BLOCK))
            if j >= i:
                row = starts[i] + (j - i) * BLOCK
                block = g_ref[row : row + BLOCK, :] / points
                work[here] = block if i == j else block.T
            else:
                work[here] = zero

    def step(k, carry):
        base = pl.multiple_of(k * BLOCK, BLOCK)
        diag[...] = work[pl.ds(base, BLOCK), pl.ds(base, BLOCK)]
        side[...] = eye
        factor_diagonal(diag, side, dinv, spread)
        corner = jnp.dot(
            dinv[...], work[pl.ds(base, BLOCK), pl.ds(base, BLOCK)],
            precision=HI, preferred_element_type=jnp.float32,
        )
        factor_ref[pl.ds(base, BLOCK), pl.ds(base, BLOCK)] = jnp.where(lane >= rank, corner, 0.0)
        work[pl.ds(base, BLOCK), pl.ds(base, BLOCK)] = eye
        panel = jnp.dot(
            dinv[...], work[pl.ds(base, BLOCK), :], precision=HI, preferred_element_type=jnp.float32
        )
        work[pl.ds(base, BLOCK), :] = panel

        def update(i, inner):
            low = pl.multiple_of(i * BLOCK, BLOCK)
            left = work[pl.ds(base, BLOCK), pl.ds(low, BLOCK)].T
            work[pl.ds(low, BLOCK), pl.ds(base, BLOCK)] = zero
            work[pl.ds(low, BLOCK), :] -= jnp.dot(
                left, work[pl.ds(base, BLOCK), :], precision=HI, preferred_element_type=jnp.float32
            )
            return inner

        lax.fori_loop(k + 1, blocks, update, 0)
        return carry

    lax.fori_loop(0, blocks, step, 0)
    for i in range(blocks):
        rows = slice(i * BLOCK, (i + 1) * BLOCK)
        for j in range(blocks):
            cols = slice(j * BLOCK, (j + 1) * BLOCK)
            if j < i:
                factor_ref[rows, cols] = zero
            elif j > i:
                factor_ref[rows, cols] = work[rows, cols]
        depth = (i + 1) * BLOCK
        part = work[rows, :depth]
        top = part.astype(jnp.bfloat16)
        rest = (part - top.astype(jnp.float32)).astype(jnp.bfloat16)
        solved = jnp.dot(top, m_ref[:depth, :], preferred_element_type=jnp.float32)
        solved = solved + jnp.dot(rest, m_ref[:depth, :], preferred_element_type=jnp.float32)
        modes_ref[rows, :] = solved.astype(jnp.bfloat16)


def factor_and_solve(gram, matrix, points):
    width, count = matrix.shape
    vmem = pl.BlockSpec(memory_space=pltpu.VMEM)
    return pl.pallas_call(
        functools.partial(solve_kernel, float(points)),
        out_shape=(
            jax.ShapeDtypeStruct((width, count), jnp.bfloat16),
            jax.ShapeDtypeStruct((width, width), jnp.float32),
        ),
        in_specs=[vmem, vmem],
        out_specs=(vmem, vmem),
        scratch_shapes=[
            pltpu.VMEM((width, width), jnp.float32),
            pltpu.VMEM((BLOCK, BLOCK), jnp.float32),
            pltpu.VMEM((BLOCK, BLOCK), jnp.float32),
            pltpu.VMEM((BLOCK, BLOCK), jnp.float32),
            pltpu.VMEM((2, 8, 8, BLOCK), jnp.float32),
        ],
        compiler_params=pltpu.CompilerParams(vmem_limit_bytes=VMEM_LIMIT),
        name="factor_solve",
    )(gram, matrix)


def body(velocity):
    planes = velocity.shape[2]
    extended = with_halo(velocity[:, 1:3], (("slab", 2),), 4)
    second_rim = extended[:, 0].astype(jnp.float32)
    third_rim = extended[:, 1].astype(jnp.float32)
    first = velocity[:, 0].astype(jnp.float32)
    second = velocity[:, 1].astype(jnp.float32)
    third = velocity[:, 2].astype(jnp.float32)
    omega_one = derive(third, 2) - derive(second, 3)
    omega_two = derive(first, 3) - differ(third_rim, 1, planes)
    omega_three = differ(second_rim, 1, planes) - derive(first, 2)
    vorticity = jnp.stack([omega_one, omega_two, omega_three], axis=1).astype(jnp.bfloat16)
    flat = vorticity.reshape(vorticity.shape[0] * 3, -1)
    snap, slab = lax.axis_size("snap"), lax.axis_size("slab")
    matrix, total = summed_gram(flat, snap, slab)
    width, rows = matrix.shape
    modes, factor = factor_and_solve(total, matrix, rows * snap * slab)
    return (modes.reshape(width, 1, rows), factor)


def solution(mesh):
    in_specs = (P("snap", None, "slab", None, None),)
    out_specs = (P(None, "slab", "snap"), P())
    return jax.shard_map(body, mesh=mesh, in_specs=in_specs, out_specs=out_specs, check_vma=False)
```
